32 devices in a mesh: atom: 4 (over y, x), mode: 8 (over z, core).
Axes of the slice: x: 2, y: 2, z: 4, core: 2. Of those that a mesh axis runs over, the one named last changes fastest.
Arguments:
- first_panel: bfloat16 [16384, 3, 1024], P('atom', None, 'mode'), may hold values from -6 to 6
- second_panel: bfloat16 [16384, 3, 1024], P('atom', None, 'mode'), may hold values from -6 to 6
- offsets: int32 [24, 16384], P(None, 'atom'), may hold values from -256 to 256, as said below
- forces: float32 [24, 3, 3, 16384], P(None, None, None, 'atom'), may hold values from -0.75 to 0.75
- displacements: float32 [24, 3, 16384], P(None, None, 'atom'), may hold values from -1 to 1
Outputs:
- velocity: float32 [1024, 3, 1024], P(('atom', 'mode'))
The draws below stay inside these ranges and needn't reach their ends.
Inputs may be any that keep to these rules, and one draw needn't show every extreme that they name: `offsets`: no entry is zero, and both 256 and -256 occur.
All inputs are finite; a program needn't handle non-finite values.
Results may differ from the reference program's by a relative error of at most 0.0041.
Values may be sent and summed in bfloat16 or wider, within the bound.
A program may use at most 192 MiB of HBM per device.

```python
import jax
import jax.numpy as jnp
from jax import lax

MODES = 1024
NBR = 24
A_DEV = 512
ATOMS = 16384
RIM = 256


def draw_offsets(key, part):
    key_size = jax.random.fold_in(key, 11)
    key_sign = jax.random.fold_in(key, 12)
    key_place = jax.random.fold_in(key, 13)
    magnitude = jax.random.randint(key_size, (NBR, ATOMS), 1, RIM + 1)
    signs = jax.random.randint(key_sign, (NBR, ATOMS), 0, 2) * 2 - 1
    shifts = (magnitude * signs).astype(jnp.int32)
    places = jax.random.randint(key_place, (2,), 0, ATOMS)
    shifts = shifts.at[0, places[0]].set(RIM)
    shifts = shifts.at[NBR - 1, places[1]].set(-RIM)
    return shifts


def levels(own_key, dims, cuts, low, high):
    def one(axis_at, parts):
        draws = jax.random.uniform(jax.random.fold_in(jax.random.fold_in(own_key, 6), axis_at), (parts,), jnp.float32, low / len(cuts), high / len(cuts))
        return jnp.repeat(jnp.exp(draws), dims[axis_at] // parts).reshape((-1,) + (1,) * (len(dims) - axis_at - 1))

    factor_of = one(*cuts[0])
    for cut in cuts[1:]:
        factor_of = factor_of * one(*cut)
    return factor_of


def scatter_about(key, dims, scale, reach, shards=(), held_as=jnp.bfloat16):
    factor_of = levels(key, dims, shards, -0.22, 0.18) if shards else 1.0
    drawn = jax.random.normal(key, dims, jnp.float32) * scale * factor_of
    return jnp.minimum(jnp.maximum(drawn, -reach), reach).astype(held_as)


def setup_inputs(seed: int = 0) -> dict:
    key_of = jax.random.split(jax.random.key(seed), 6)
    first_panel = scatter_about(key_of[0], (ATOMS, 3, MODES), 1.0, 6.0, ((0, 4), (2, 8)))
    second_panel = scatter_about(key_of[1], (ATOMS, 3, MODES), 1.0, 6.0, ((0, 4), (2, 8)))
    offsets = draw_offsets(jax.random.fold_in(key_of[5], 71), 0)
    forces = scatter_about(key_of[3], (NBR, 3, 3, ATOMS), (3 * NBR) ** -0.5, 0.75, ((3, 4),), jnp.float32)
    displacements = jnp.clip(jax.random.uniform(key_of[4], (NBR, 3, ATOMS), jnp.float32, -1.0, 1.0) * levels(key_of[4], (NBR, 3, ATOMS), ((2, 4),), -0.4, 0.0), -1.0, 1.0)
    return dict(first_panel=first_panel, second_panel=second_panel, offsets=offsets, forces=forces, displacements=displacements)


def reference(first_panel, second_panel, offsets, forces, displacements):
    def one_block(running, number):
        row_start = (number * A_DEV).astype(jnp.int32)
        indices = row_start + jnp.arange(A_DEV, dtype=jnp.int32)
        shifts = lax.dynamic_slice_in_dim(offsets, row_start, A_DEV, 1)
        partner = (indices[None, :] + shifts) % ATOMS
        gathered = second_panel[partner].astype(jnp.float32)
        force_part = lax.dynamic_slice_in_dim(forces, row_start, A_DEV, 3)
        disp_part = lax.dynamic_slice_in_dim(displacements, row_start, A_DEV, 2)
        blocks = (disp_part[:, :, None, None, :] * force_part[:, None, :, :, :]).astype(jnp.bfloat16)
        images = jnp.einsum("kqabi,kibn->iqan", blocks.astype(jnp.float32), gathered).astype(jnp.bfloat16)
        panel_rows = lax.dynamic_slice_in_dim(first_panel, row_start, A_DEV, 0).astype(jnp.float32)
        partial_value = jnp.einsum("iam,iqan->mqn", panel_rows, images.astype(jnp.float32))
        return running + partial_value, None

    start_sum = jnp.zeros((MODES, 3, MODES), jnp.float32)
    running, unused = lax.scan(one_block, start_sum, jnp.arange(ATOMS // A_DEV, dtype=jnp.int32))
    return running * (1.0 / (3.0 * ATOMS) ** 0.5)
```

```python
import functools

import jax
import jax.numpy as jnp
from jax import lax
from jax.experimental import pallas as pl
from jax.experimental.pallas import tpu as pltpu
from jax.sharding import PartitionSpec as P

RIM = 256
BLOCK = 128
CHUNK = 64
MESH = pl.DeviceIdType.MESH


def with_rims(block, width):
    axes = ("atom", "mode")
    count = lax.axis_size(axes)
    forward = [(i, (i + 1) % count) for i in range(count)]
    backward = [(target, source) for source, target in forward]
    low = lax.ppermute(block[:, block.shape[1] - width :], axes, forward)
    high = lax.ppermute(block[:, :width], axes, backward)
    return jnp.concatenate([low, block, high], axis=1)


def merged_blocks(offsets, forces, displacements):
    slots, rows = offsets.shape
    blocks = displacements[:, :, None, None, :] * forces[:, None, :, :, :]
    blocks = blocks.astype(jnp.bfloat16).astype(jnp.float32).reshape(slots, 9, 3, rows)
    same = offsets[:, None, :] == offsets[None, :, :]
    merged = jnp.sum(
        jnp.where(same[:, :, None, None, :], blocks[None], 0.0), axis=1
    )
    return merged.transpose(1, 0, 2, 3).reshape(9, slots * 3, rows)


def image_kernel(slots, offs_ref, coef_ref, s_ref, out_ref, w_ref):
    window = BLOCK + 2 * RIM
    start = pl.multiple_of(pl.program_id(0) * BLOCK, BLOCK)
    target = offs_ref[...] + lax.broadcasted_iota(jnp.int32, offs_ref.shape, 1) + RIM
    rows = lax.broadcasted_iota(jnp.int32, (CHUNK, BLOCK), 0)

    for qa in range(9):

        @pl.loop(0, window // CHUNK)
        def _(c):
            at = pl.multiple_of(c * CHUNK, CHUNK)
            here = rows + at
            acc = [jnp.zeros((CHUNK, BLOCK), jnp.float32) for _ in range(3)]
            for k in range(slots):
                hit = here == target[k : k + 1, :]
                for b in range(3):
                    row = coef_ref[qa, 3 * k + b : 3 * k + b + 1, :]
                    acc[b] = jnp.where(hit, row, acc[b])
            for b in range(3):
                w_ref[b, pl.ds(at, CHUNK), qa * BLOCK : (qa + 1) * BLOCK] = acc[b].astype(
                    jnp.bfloat16
                )

    columns = s_ref.shape[2]
    wide = 512

    @pl.loop(0, columns // wide)
    def _(c):
        at = pl.multiple_of(c * wide, wide)
        total = None
        for b in range(3):
            term = lax.dot_general(
                w_ref[b],
                s_ref[b, pl.ds(start, window), pl.ds(at, wide)],
                (((0,), (0,)), ((), ())),
                preferred_element_type=jnp.float32,
            )
            total = term if total is None else total + term
        out_ref[:, :, pl.ds(at, wide)] = total.astype(jnp.bfloat16).reshape(9, BLOCK, wide)


def make_images(padded, offs, coef):
    slots, rows = offs.shape
    columns = padded.shape[2]
    window = BLOCK + 2 * RIM
    return pl.pallas_call(
        functools.partial(image_kernel, slots),
        grid=(rows // BLOCK,),
        out_shape=jax.ShapeDtypeStruct((9, rows, columns), jnp.bfloat16),
        in_specs=[
            pl.BlockSpec((slots, BLOCK), lambda i: (0, i)),
            pl.BlockSpec((9, slots * 3, BLOCK), lambda i: (0, 0, i)),
            pl.BlockSpec(memory_space=pltpu.VMEM),
        ],
        out_specs=pl.BlockSpec((9, BLOCK, columns), lambda i: (0, i, 0)),
        scratch_shapes=[pltpu.VMEM((3, window, 9 * BLOCK), jnp.bfloat16)],
        compiler_params=pltpu.CompilerParams(vmem_limit_bytes=56 * 2**20),
        cost_estimate=pl.CostEstimate(
            flops=2 * 27 * rows * window * columns,
            bytes_accessed=9 * rows * columns * 2,
            transcendentals=0,
        ),
        name="images",
    )(offs, coef, padded)


def reduce_kernel(
    scale, n_atom, n_half, f_ref, img_ref, out_ref,
    part, core_in, atom_out, atom_in, z_out, z_in,
    core_send, core_recv, atom_send, atom_recv, z_send, z_recv,
):
    me_atom = lax.axis_index("atom")
    me_mode = lax.axis_index("mode")
    core = lax.rem(me_mode, 2)
    me_z = me_mode // 2
    other = me_z * 2 + 1 - core
    own = out_ref.shape[0]
    columns = img_ref.shape[3]
    chunk = n_half * 2 * own

    barrier = pltpu.get_barrier_semaphore()
    pl.semaphore_signal(barrier, inc=1, device_id=(me_atom, other), device_id_type=MESH)
    for s in range(1, n_atom):
        to = lax.rem(me_atom + s, n_atom)
        pl.semaphore_signal(barrier, inc=1, device_id=(to, me_mode), device_id_type=MESH)
    for s in range(1, n_half):
        to = lax.rem(me_z + s, n_half) * 2 + core
        pl.semaphore_signal(barrier, inc=1, device_id=(me_atom, to), device_id_type=MESH)
    pl.semaphore_wait(barrier, n_atom + n_half - 1)

    core_copies, atom_copies = [], []

    def multiply(s):
        a_to = lax.rem(me_atom + 1 + s, n_atom)

        @pl.loop(0, 3)
        def _(q):
            total = None
            for a in range(3):
                term = lax.dot_general(
                    f_ref[a, :, pl.ds(pl.multiple_of(a_to * chunk, chunk), chunk)],
                    img_ref[q, a],
                    (((0,), (0,)), ((), ())),
                    preferred_element_type=jnp.float32,
                )
                total = term if total is None else total + term
            total = (total * scale).astype(part.dtype)
            part[s, q] = total.reshape(n_half, 2, own, columns)

        copy = pltpu.make_async_remote_copy(
            src_ref=part.at[s, :, :, 1 - core],
            dst_ref=core_in.at[s],
            send_sem=core_send.at[s],
            recv_sem=core_recv.at[s],
            device_id=(me_atom, other),
            device_id_type=MESH,
        )
        copy.start()
        core_copies.append(copy)

    def combine(s):
        core_copies[s].wait_recv()

        @pl.loop(0, n_half)
        def _(h):
            for q in range(3):
                mine = part[s, q, h, core].astype(jnp.float32)
                atom_out[s, q, h] = (mine + core_in[s, q, h].astype(jnp.float32)).astype(
                    atom_out.dtype
                )

        if s < n_atom - 1:
            a_to = lax.rem(me_atom + 1 + s, n_atom)
            copy = pltpu.make_async_remote_copy(
                src_ref=atom_out.at[s],
                dst_ref=atom_in.at[s],
                send_sem=atom_send.at[s],
                recv_sem=atom_recv.at[s],
                device_id=(a_to, me_mode),
                device_id_type=MESH,
            )
            copy.start()
            atom_copies.append(copy)

    for s in range(n_atom):
        multiply(s)
        if s >= 1:
            combine(s - 1)
    combine(n_atom - 1)

    for copy in atom_copies:
        copy.wait_recv()
    z_copies = []
    for s in range(n_half):
        h = lax.rem(me_z + 1 + s, n_half)
        for q in range(3):
            total = atom_out[n_atom - 1, q, h].astype(jnp.float32)
            for t in range(n_atom - 1):
                total = total + atom_in[t, q, h].astype(jnp.float32)
            z_out[s, q] = total.astype(z_out.dtype)
        if s < n_half - 1:
            copy = pltpu.make_async_remote_copy(
                src_ref=z_out.at[s],
                dst_ref=z_in.at[s],
                send_sem=z_send.at[s],
                recv_sem=z_recv.at[s],
                device_id=(me_atom, h * 2 + core),
                device_id_type=MESH,
            )
            copy.start()
            z_copies.append(copy)
    for copy in z_copies:
        copy.wait_recv()
    for q in range(3):
        total = z_out[n_half - 1, q].astype(jnp.float32)
        for t in range(n_half - 1):
            total = total + z_in[t, q].astype(jnp.float32)
        out_ref[:, q * columns : (q + 1) * columns] = total
    for copy in core_copies + atom_copies + z_copies:
        copy.wait_send()


def multiply_and_reduce(panel, images, scale):
    n_atom = lax.axis_size("atom")
    n_half = lax.axis_size("mode") // 2
    modes = panel.shape[2]
    columns = images.shape[2]
    rows = panel.shape[1]
    own = modes // (n_atom * n_half * 2)
    wire = jnp.bfloat16 if own % 16 == 0 else jnp.float32
    images = images.reshape(3, 3, rows, columns)
    vmem = pl.BlockSpec(memory_space=pltpu.VMEM)
    dma = pltpu.SemaphoreType.DMA
    out = pl.pallas_call(
        functools.partial(reduce_kernel, scale, n_atom, n_half),
        out_shape=jax.ShapeDtypeStruct((own, 3 * columns), jnp.float32),
        in_specs=[vmem, vmem],
        out_specs=vmem,
        scratch_shapes=[
            pltpu.VMEM((n_atom, 3, n_half, 2, own, columns), wire),
            pltpu.VMEM((n_atom, 3, n_half, own, columns), wire),
            pltpu.VMEM((n_atom, 3, n_half, own, columns), wire),
            pltpu.VMEM((n_atom - 1, 3, n_half, own, columns), wire),
            pltpu.VMEM((n_half, 3, own, columns), wire),
            pltpu.VMEM((n_half - 1, 3, own, columns), wire),
            dma((n_atom,)),
            dma((n_atom,)),
            dma((n_atom - 1,)),
            dma((n_atom - 1,)),
            dma((n_half - 1,)),
            dma((n_half - 1,)),
        ],
        compiler_params=pltpu.CompilerParams(
            collective_id=0, has_side_effects=True, vmem_limit_bytes=60 * 2**20
        ),
        cost_estimate=pl.CostEstimate(
            flops=2 * 9 * rows * modes * columns,
            bytes_accessed=9 * rows * columns * 2,
            transcendentals=0,
        ),
        name="reduce",
    )(panel, images)
    return out.reshape(own, 3, columns)


def body(first_panel, second_panel, offsets, forces, displacements):
    groups = lax.axis_size("mode")
    rows_dev = first_panel.shape[0] // groups
    atoms_all = first_panel.shape[0] * lax.axis_size("atom")
    scale = 1.0 / (3.0 * atoms_all) ** 0.5
    second_rows = lax.all_to_all(
        second_panel.transpose(1, 0, 2), "mode", split_axis=1, concat_axis=2, tiled=True
    )
    ordered, second_rows = lax.optimization_barrier((first_panel.transpose(1, 0, 2), second_rows))
    panel_rows = lax.all_to_all(ordered, "mode", split_axis=1, concat_axis=2, tiled=True)
    padded = with_rims(second_rows, RIM)
    row_start = lax.axis_index("mode") * rows_dev
    shifts = lax.dynamic_slice_in_dim(offsets, row_start, rows_dev, 1)
    force_part = lax.dynamic_slice_in_dim(forces, row_start, rows_dev, 3)
    disp_part = lax.dynamic_slice_in_dim(displacements, row_start, rows_dev, 2)
    coef = merged_blocks(shifts, force_part, disp_part)
    images = make_images(padded, shifts, coef)
    return multiply_and_reduce(panel_rows, images, scale)


def solution(mesh):
    in_specs = (
        P("atom", None, "mode"),
        P("atom", None, "mode"),
        P(None, "atom"),
        P(None, None, None, "atom"),
        P(None, None, "atom"),
    )
    out_specs = P(("atom", "mode"), None, None)
    return jax.shard_map(body, mesh=mesh, in_specs=in_specs, out_specs=out_specs, check_vma=False)
```

```python
import functools

import jax
import jax.numpy as jnp
from jax import lax
from jax.experimental import pallas as pl
from jax.experimental.pallas import tpu as pltpu
from jax.sharding import PartitionSpec as P

RIM = 256
BLOCK = 128
CHUNK = 64
MESH = pl.DeviceIdType.MESH


def with_rims(block, width):
    axes = ("atom", "mode")
    count = lax.axis_size(axes)
    forward = [(i, (i + 1) % count) for i in range(count)]
    backward = [(target, source) for source, target in forward]
    low = lax.ppermute(block[:, block.shape[1] - width :], axes, forward)
    high = lax.ppermute(block[:, :width], axes, backward)
    return jnp.concatenate([low, block, high], axis=1)


def merged_blocks(offsets, forces, displacements):
    slots, rows = offsets.shape
    blocks = displacements[:, :, None, None, :] * forces[:, None, :, :, :]
    blocks = blocks.astype(jnp.bfloat16).astype(jnp.float32).reshape(slots, 9, 3, rows)
    same = offsets[:, None, :] == offsets[None, :, :]
    merged = jnp.sum(
        jnp.where(same[:, :, None, None, :], blocks[None], 0.0), axis=1
    )
    return merged.transpose(1, 0, 2, 3).reshape(9, slots * 3, rows)


def image_kernel(slots, offs_ref, coef_ref, s_ref, out_ref, w_ref):
    window = BLOCK + 2 * RIM
    start = pl.multiple_of(pl.program_id(0) * BLOCK, BLOCK)
    target = offs_ref[...] + lax.broadcasted_iota(jnp.int32, offs_ref.shape, 1) + RIM
    rows = lax.broadcasted_iota(jnp.int32, (CHUNK, BLOCK), 0)

    for qa in range(9):

        @pl.loop(0, window // CHUNK)
        def _(c):
            at = pl.multiple_of(c * CHUNK, CHUNK)
            here = rows + at
            acc = [jnp.zeros((CHUNK, BLOCK), jnp.float32) for _ in range(3)]
            for k in range(slots):
                hit = here == target[k : k + 1, :]
                for b in range(3):
                    row = coef_ref[qa, 3 * k + b : 3 * k + b + 1, :]
                    acc[b] = jnp.where(hit, row, acc[b])
            for b in range(3):
                w_ref[b, pl.ds(at, CHUNK), qa * BLOCK : (qa + 1) * BLOCK] = acc[b].astype(
                    jnp.bfloat16
                )

    columns = s_ref.shape[2]
    wide = 512

    @pl.loop(0, columns // wide)
    def _(c):
        at = pl.multiple_of(c * wide, wide)
        total = None
        for b in range(3):
            term = lax.dot_general(
                w_ref[b],
                s_ref[b, pl.ds(start, window), pl.ds(at, wide)],
                (((0,), (0,)), ((), ())),
                preferred_element_type=jnp.float32,
            )
            total = term if total is None else total + term
        out_ref[:, :, pl.ds(at, wide)] = total.astype(jnp.bfloat16).reshape(9, BLOCK, wide)


def make_images(padded, offs, coef):
    slots, rows = offs.shape
    columns = padded.shape[2]
    window = BLOCK + 2 * RIM
    return pl.pallas_call(
        functools.partial(image_kernel, slots),
        grid=(rows // BLOCK,),
        out_shape=jax.ShapeDtypeStruct((9, rows, columns), jnp.bfloat16),
        in_specs=[
            pl.BlockSpec((slots, BLOCK), lambda i: (0, i)),
            pl.BlockSpec((9, slots * 3, BLOCK), lambda i: (0, 0, i)),
            pl.BlockSpec(memory_space=pltpu.VMEM),
        ],
        out_specs=pl.BlockSpec((9, BLOCK, columns), lambda i: (0, i, 0)),
        scratch_shapes=[pltpu.VMEM((3, window, 9 * BLOCK), jnp.bfloat16)],
        compiler_params=pltpu.CompilerParams(vmem_limit_bytes=56 * 2**20),
        cost_estimate=pl.CostEstimate(
            flops=2 * 27 * rows * window * columns,
            bytes_accessed=9 * rows * columns * 2,
            transcendentals=0,
        ),
        name="images",
    )(offs, coef, padded)


def reduce_kernel(
    scale, n_atom, n_half, f_ref, img_ref, out_ref,
    part, core_in, atom_out, atom_in, z_out, z_in,
    core_send, core_recv, atom_send, atom_recv, z_send, z_recv,
):
    me_atom = lax.axis_index("atom")
    me_mode = lax.axis_index("mode")
    core = lax.rem(me_mode, 2)
    me_z = me_mode // 2
    other = me_z * 2 + 1 - core
    own = out_ref.shape[1]
    columns = img_ref.shape[3]
    chunk = n_half * 2 * own

    barrier = pltpu.get_barrier_semaphore()
    pl.semaphore_signal(barrier, inc=1, device_id=(me_atom, other), device_id_type=MESH)
    for s in range(1, n_atom):
        to = lax.rem(me_atom + s, n_atom)
        pl.semaphore_signal(barrier, inc=1, device_id=(to, me_mode), device_id_type=MESH)
    for s in range(1, n_half):
        to = lax.rem(me_z + s, n_half) * 2 + core
        pl.semaphore_signal(barrier, inc=1, device_id=(me_atom, to), device_id_type=MESH)
    pl.semaphore_wait(barrier, n_atom + n_half - 1)

    core_copies, atom_copies = [], []

    def multiply(s):
        a_to = lax.rem(me_atom + 1 + s, n_atom)

        @pl.loop(0, 3)
        def _(q):
            total = None
            for a in range(3):
                term = lax.dot_general(
                    f_ref[a, :, pl.ds(pl.multiple_of(a_to * chunk, chunk), chunk)],
                    img_ref[q, a],
                    (((0,), (0,)), ((), ())),
                    preferred_element_type=jnp.float32,
                )
                total = term if total is None else total + term
            total = (total * scale).astype(part.dtype)
            part[s, q] = total.reshape(n_half, 2, own, columns)

        copy = pltpu.make_async_remote_copy(
            src_ref=part.at[s, :, :, 1 - core],
            dst_ref=core_in.at[s],
            send_sem=core_send.at[s],
            recv_sem=core_recv.at[s],
            device_id=(me_atom, other),
            device_id_type=MESH,
        )
        copy.start()
        core_copies.append(copy)

    def combine(s):
        core_copies[s].wait_recv()

        @pl.loop(0, n_half)
        def _(h):
            for q in range(3):
                mine = part[s, q, h, core].astype(jnp.float32)
                atom_out[s, q, h] = (mine + core_in[s, q, h].astype(jnp.float32)).astype(
                    atom_out.dtype
                )

        if s < n_atom - 1:
            a_to = lax.rem(me_atom + 1 + s, n_atom)
            copy = pltpu.make_async_remote_copy(
                src_ref=atom_out.at[s],
                dst_ref=atom_in.at[s],
                send_sem=atom_send.at[s],
                recv_sem=atom_recv.at[s],
                device_id=(a_to, me_mode),
                device_id_type=MESH,
            )
            copy.start()
            atom_copies.append(copy)

    for s in range(n_atom):
        multiply(s)
        if s >= 1:
            combine(s - 1)
    combine(n_atom - 1)

    for copy in atom_copies:
        copy.wait_recv()
    z_copies = []
    for s in range(n_half):
        h = lax.rem(me_z + 1 + s, n_half)
        for q in range(3):
            total = atom_out[n_atom - 1, q, h].astype(jnp.float32)
            for t in range(n_atom - 1):
                total = total + atom_in[t, q, h].astype(jnp.float32)
            z_out[s, q] = total.astype(z_out.dtype)
        if s < n_half - 1:
            copy = pltpu.make_async_remote_copy(
                src_ref=z_out.at[s],
                dst_ref=z_in.at[s],
                send_sem=z_send.at[s],
                recv_sem=z_recv.at[s],
                device_id=(me_atom, h * 2 + core),
                device_id_type=MESH,
            )
            copy.start()
            z_copies.append(copy)
    for copy in z_copies:
        copy.wait_recv()
    for q in range(3):
        total = z_out[n_half - 1, q].astype(jnp.float32)
        for t in range(n_half - 1):
            total = total + z_in[t, q].astype(jnp.float32)
        out_ref[q] = total
    for copy in core_copies + atom_copies + z_copies:
        copy.wait_send()


def multiply_and_reduce(panel, images, scale):
    n_atom = lax.axis_size("atom")
    n_half = lax.axis_size("mode") // 2
    modes = panel.shape[2]
    columns = images.shape[2]
    rows = panel.shape[1]
    own = modes // (n_atom * n_half * 2)
    wire = jnp.bfloat16 if own % 16 == 0 else jnp.float32
    images = images.reshape(3, 3, rows, columns)
    vmem = pl.BlockSpec(memory_space=pltpu.VMEM)
    dma = pltpu.SemaphoreType.DMA
    out = pl.pallas_call(
        functools.partial(reduce_kernel, scale, n_atom, n_half),
        out_shape=jax.ShapeDtypeStruct((3, own, columns), jnp.float32),
        in_specs=[vmem, vmem],
        out_specs=vmem,
        scratch_shapes=[
            pltpu.VMEM((n_atom, 3, n_half, 2, own, columns), wire),
            pltpu.VMEM((n_atom, 3, n_half, own, columns), wire),
            pltpu.VMEM((n_atom, 3, n_half, own, columns), wire),
            pltpu.VMEM((n_atom - 1, 3, n_half, own, columns), wire),
            pltpu.VMEM((n_half, 3, own, columns), wire),
            pltpu.VMEM((n_half - 1, 3, own, columns), wire),
            dma((n_atom,)),
            dma((n_atom,)),
            dma((n_atom - 1,)),
            dma((n_atom - 1,)),
            dma((n_half - 1,)),
            dma((n_half - 1,)),
        ],
        compiler_params=pltpu.CompilerParams(
            collective_id=0, has_side_effects=True, vmem_limit_bytes=60 * 2**20
        ),
        cost_estimate=pl.CostEstimate(
            flops=2 * 9 * rows * modes * columns,
            bytes_accessed=9 * rows * columns * 2,
            transcendentals=0,
        ),
        name="reduce",
    )(panel, images)
    return out.transpose(1, 0, 2)


def body(first_panel, second_panel, offsets, forces, displacements):
    groups = lax.axis_size("mode")
    rows_dev = first_panel.shape[0] // groups
    atoms_all = first_panel.shape[0] * lax.axis_size("atom")
    scale = 1.0 / (3.0 * atoms_all) ** 0.5
    second_rows = lax.all_to_all(
        second_panel.transpose(1, 0, 2), "mode", split_axis=1, concat_axis=2, tiled=True
    )
    padded = with_rims(second_rows, RIM)
    ordered, padded = lax.optimization_barrier((first_panel.transpose(1, 0, 2), padded))
    panel_rows = lax.all_to_all(ordered, "mode", split_axis=1, concat_axis=2, tiled=True)
    row_start = lax.axis_index("mode") * rows_dev
    shifts = lax.dynamic_slice_in_dim(offsets, row_start, rows_dev, 1)
    force_part = lax.dynamic_slice_in_dim(forces, row_start, rows_dev, 3)
    disp_part = lax.dynamic_slice_in_dim(displacements, row_start, rows_dev, 2)
    coef = merged_blocks(shifts, force_part, disp_part)
    images = make_images(padded, shifts, coef)
    return multiply_and_reduce(panel_rows, images, scale)


def solution(mesh):
    in_specs = (
        P("atom", None, "mode"),
        P("atom", None, "mode"),
        P(None, "atom"),
        P(None, None, None, "atom"),
        P(None, None, "atom"),
    )
    out_specs = P(("atom", "mode"), None, None)
    return jax.shard_map(body, mesh=mesh, in_specs=in_specs, out_specs=out_specs, check_vma=False)
```

```python
import functools

import jax
import jax.numpy as jnp
from jax import lax
from jax.experimental import pallas as pl
from jax.experimental.pallas import tpu as pltpu
from jax.sharding import PartitionSpec as P

RIM = 256
BLOCK = 128
CHUNK = 64
MESH = pl.DeviceIdType.MESH


def with_rims(block, width):
    axes = ("atom", "mode")
    count = lax.axis_size(axes)
    forward = [(i, (i + 1) % count) for i in range(count)]
    backward = [(target, source) for source, target in forward]
    low = lax.ppermute(block[:, block.shape[1] - width :], axes, forward)
    high = lax.ppermute(block[:, :width], axes, backward)
    return jnp.concatenate([low, block, high], axis=1)


def exchange_kernel(
    n_atom, groups, s_ref, out_ref, send, recv, rim_send, rim_recv, local
):
    me_atom = lax.axis_index("atom")
    me = lax.axis_index("mode")
    width = s_ref.shape[2]
    rows = s_ref.shape[1] // groups
    number = me_atom * groups + me
    count = n_atom * groups
    after = lax.rem(number + 1, count)
    before = lax.rem(number + count - 1, count)
    after = (after // groups, lax.rem(after, groups))
    before = (before // groups, lax.rem(before, groups))

    barrier = pltpu.get_barrier_semaphore()
    for s in range(1, groups):
        to = lax.rem(me + s, groups)
        pl.semaphore_signal(barrier, inc=1, device_id=(me_atom, to), device_id_type=MESH)
    pl.semaphore_signal(barrier, inc=1, device_id=after, device_id_type=MESH)
    pl.semaphore_signal(barrier, inc=1, device_id=before, device_id_type=MESH)
    pl.semaphore_wait(barrier, groups + 1)

    columns = pl.ds(pl.multiple_of(me * width, width), width)
    landing = out_ref.at[:, pl.ds(RIM, rows), columns]
    copies = []
    for s in range(1, groups):
        to = lax.rem(me + s, groups)
        copy = pltpu.make_async_remote_copy(
            src_ref=s_ref.at[:, pl.ds(pl.multiple_of(to * rows, rows), rows), :],
            dst_ref=landing,
            send_sem=send.at[s - 1],
            recv_sem=recv.at[s - 1],
            device_id=(me_atom, to),
            device_id_type=MESH,
        )
        copy.start()
        copies.append(copy)
    mine = pltpu.make_async_copy(
        s_ref.at[:, pl.ds(pl.multiple_of(me * rows, rows), rows), :], landing, local
    )
    mine.start()
    mine.wait()
    for copy in copies:
        copy.wait_recv()

    rims = []
    for at, (source, target, device) in enumerate(
        ((rows, 0, after), (RIM, RIM + rows, before))
    ):
        copy = pltpu.make_async_remote_copy(
            src_ref=out_ref.at[:, pl.ds(source, RIM), :],
            dst_ref=out_ref.at[:, pl.ds(target, RIM), :],
            send_sem=rim_send.at[at],
            recv_sem=rim_recv.at[at],
            device_id=device,
            device_id_type=MESH,
        )
        copy.start()
        rims.append(copy)
    for copy in rims:
        copy.wait_recv()
    for copy in copies + rims:
        copy.wait_send()


def exchange_with_rims(panel):
    n_atom, groups = lax.axis_size("atom"), lax.axis_size("mode")
    rows, width = panel.shape[1] // groups, panel.shape[2]
    if width % 128:
        whole = lax.all_to_all(panel, "mode", split_axis=1, concat_axis=2, tiled=True)
        return with_rims(whole, RIM)
    dma = pltpu.SemaphoreType.DMA
    return pl.pallas_call(
        functools.partial(exchange_kernel, n_atom, groups),
        out_shape=jax.ShapeDtypeStruct((3, rows + 2 * RIM, width * groups), panel.dtype),
        in_specs=[pl.BlockSpec(memory_space=pl.ANY)],
        out_specs=pl.BlockSpec(memory_space=pl.ANY),
        scratch_shapes=[dma((groups - 1,)), dma((groups - 1,)), dma((2,)), dma((2,)), dma],
        compiler_params=pltpu.CompilerParams(collective_id=1, has_side_effects=True),
        name="exchange",
    )(panel)


def merged_blocks(offsets, forces, displacements):
    slots, rows = offsets.shape
    blocks = displacements[:, :, None, None, :] * forces[:, None, :, :, :]
    blocks = blocks.astype(jnp.bfloat16).astype(jnp.float32).reshape(slots, 9, 3, rows)
    same = offsets[:, None, :] == offsets[None, :, :]
    merged = jnp.sum(
        jnp.where(same[:, :, None, None, :], blocks[None], 0.0), axis=1
    )
    return merged.transpose(1, 0, 2, 3).reshape(9, slots * 3, rows)


def image_kernel(slots, offs_ref, coef_ref, s_ref, out_ref, w_ref):
    window = BLOCK + 2 * RIM
    start = pl.multiple_of(pl.program_id(0) * BLOCK, BLOCK)
    target = offs_ref[...] + lax.broadcasted_iota(jnp.int32, offs_ref.shape, 1) + RIM
    rows = lax.broadcasted_iota(jnp.int32, (CHUNK, BLOCK), 0)

    for qa in range(9):

        @pl.loop(0, window // CHUNK)
        def _(c):
            at = pl.multiple_of(c * CHUNK, CHUNK)
            here = rows + at
            acc = [jnp.zeros((CHUNK, BLOCK), jnp.float32) for _ in range(3)]
            for k in range(slots):
                hit = here == target[k : k + 1, :]
                for b in range(3):
                    row = coef_ref[qa, 3 * k + b : 3 * k + b + 1, :]
                    acc[b] = jnp.where(hit, row, acc[b])
            for b in range(3):
                w_ref[b, pl.ds(at, CHUNK), qa * BLOCK : (qa + 1) * BLOCK] = acc[b].astype(
                    jnp.bfloat16
                )

    columns = s_ref.shape[2]
    wide = 512

    @pl.loop(0, columns // wide)
    def _(c):
        at = pl.multiple_of(c * wide, wide)
        total = None
        for b in range(3):
            term = lax.dot_general(
                w_ref[b],
                s_ref[b, pl.ds(start, window), pl.ds(at, wide)],
                (((0,), (0,)), ((), ())),
                preferred_element_type=jnp.float32,
            )
            total = term if total is None else total + term
        out_ref[:, :, pl.ds(at, wide)] = total.astype(jnp.bfloat16).reshape(9, BLOCK, wide)


def make_images(padded, offs, coef):
    slots, rows = offs.shape
    columns = padded.shape[2]
    window = BLOCK + 2 * RIM
    return pl.pallas_call(
        functools.partial(image_kernel, slots),
        grid=(rows // BLOCK,),
        out_shape=jax.ShapeDtypeStruct((9, rows, columns), jnp.bfloat16),
        in_specs=[
            pl.BlockSpec((slots, BLOCK), lambda i: (0, i)),
            pl.BlockSpec((9, slots * 3, BLOCK), lambda i: (0, 0, i)),
            pl.BlockSpec(memory_space=pltpu.VMEM),
        ],
        out_specs=pl.BlockSpec((9, BLOCK, columns), lambda i: (0, i, 0)),
        scratch_shapes=[pltpu.VMEM((3, window, 9 * BLOCK), jnp.bfloat16)],
        compiler_params=pltpu.CompilerParams(vmem_limit_bytes=56 * 2**20),
        cost_estimate=pl.CostEstimate(
            flops=2 * 27 * rows * window * columns,
            bytes_accessed=9 * rows * columns * 2,
            transcendentals=0,
        ),
        name="images",
    )(offs, coef, padded)


def reduce_kernel(
    scale, n_atom, n_half, f_ref, img_ref, out_ref,
    part, core_in, atom_out, atom_in, z_out, z_in,
    core_send, core_recv, atom_send, atom_recv, z_send, z_recv,
):
    me_atom = lax.axis_index("atom")
    me_mode = lax.axis_index("mode")
    core = lax.rem(me_mode, 2)
    me_z = me_mode // 2
    other = me_z * 2 + 1 - core
    own = out_ref.shape[1]
    columns = img_ref.shape[3]
    chunk = n_half * 2 * own

    barrier = pltpu.get_barrier_semaphore()
    pl.semaphore_signal(barrier, inc=1, device_id=(me_atom, other), device_id_type=MESH)
    for s in range(1, n_atom):
        to = lax.rem(me_atom + s, n_atom)
        pl.semaphore_signal(barrier, inc=1, device_id=(to, me_mode), device_id_type=MESH)
    for s in range(1, n_half):
        to = lax.rem(me_z + s, n_half) * 2 + core
        pl.semaphore_signal(barrier, inc=1, device_id=(me_atom, to), device_id_type=MESH)
    pl.semaphore_wait(barrier, n_atom + n_half - 1)

    core_copies, atom_copies = [], []

    def multiply(s):
        a_to = lax.rem(me_atom + 1 + s, n_atom)

        @pl.loop(0, 3)
        def _(q):
            total = None
            for a in range(3):
                term = lax.dot_general(
                    f_ref[a, :, pl.ds(pl.multiple_of(a_to * chunk, chunk), chunk)],
                    img_ref[q, a],
                    (((0,), (0,)), ((), ())),
                    preferred_element_type=jnp.float32,
                )
                total = term if total is None else total + term
            total = (total * scale).astype(part.dtype)
            part[s, q] = total.reshape(n_half, 2, own, columns)

        copy = pltpu.make_async_remote_copy(
            src_ref=part.at[s, :, :, 1 - core],
            dst_ref=core_in.at[s],
            send_sem=core_send.at[s],
            recv_sem=core_recv.at[s],
            device_id=(me_atom, other),
            device_id_type=MESH,
        )
        copy.start()
        core_copies.append(copy)

    def combine(s):
        core_copies[s].wait_recv()

        @pl.loop(0, n_half)
        def _(h):
            for q in range(3):
                mine = part[s, q, h, core].astype(jnp.float32)
                atom_out[s, q, h] = (mine + core_in[s, q, h].astype(jnp.float32)).astype(
                    atom_out.dtype
                )

        if s < n_atom - 1:
            a_to = lax.rem(me_atom + 1 + s, n_atom)
            copy = pltpu.make_async_remote_copy(
                src_ref=atom_out.at[s],
                dst_ref=atom_in.at[s],
                send_sem=atom_send.at[s],
                recv_sem=atom_recv.at[s],
                device_id=(a_to, me_mode),
                device_id_type=MESH,
            )
            copy.start()
            atom_copies.append(copy)

    for s in range(n_atom):
        multiply(s)
        if s >= 1:
            combine(s - 1)
    combine(n_atom - 1)

    for copy in atom_copies:
        copy.wait_recv()
    z_copies = []
    for s in range(n_half):
        h = lax.rem(me_z + 1 + s, n_half)
        for q in range(3):
            total = atom_out[n_atom - 1, q, h].astype(jnp.float32)
            for t in range(n_atom - 1):
                total = total + atom_in[t, q, h].astype(jnp.float32)
            z_out[s, q] = total.astype(z_out.dtype)
        if s < n_half - 1:
            copy = pltpu.make_async_remote_copy(
                src_ref=z_out.at[s],
                dst_ref=z_in.at[s],
                send_sem=z_send.at[s],
                recv_sem=z_recv.at[s],
                device_id=(me_atom, h * 2 + core),
                device_id_type=MESH,
            )
            copy.start()
            z_copies.append(copy)
    for copy in z_copies:
        copy.wait_recv()
    for q in range(3):
        total = z_out[n_half - 1, q].astype(jnp.float32)
        for t in range(n_half - 1):
            total = total + z_in[t, q].astype(jnp.float32)
        out_ref[q] = total
    for copy in core_copies + atom_copies + z_copies:
        copy.wait_send()


def multiply_and_reduce(panel, images, scale):
    n_atom = lax.axis_size("atom")
    n_half = lax.axis_size("mode") // 2
    modes = panel.shape[2]
    columns = images.shape[2]
    rows = panel.shape[1]
    own = modes // (n_atom * n_half * 2)
    wire = jnp.bfloat16 if own % 16 == 0 else jnp.float32
    images = images.reshape(3, 3, rows, columns)
    vmem = pl.BlockSpec(memory_space=pltpu.VMEM)
    dma = pltpu.SemaphoreType.DMA
    out = pl.pallas_call(
        functools.partial(reduce_kernel, scale, n_atom, n_half),
        out_shape=jax.ShapeDtypeStruct((3, own, columns), jnp.float32),
        in_specs=[vmem, vmem],
        out_specs=vmem,
        scratch_shapes=[
            pltpu.VMEM((n_atom, 3, n_half, 2, own, columns), wire),
            pltpu.VMEM((n_atom, 3, n_half, own, columns), wire),
            pltpu.VMEM((n_atom, 3, n_half, own, columns), wire),
            pltpu.VMEM((n_atom - 1, 3, n_half, own, columns), wire),
            pltpu.VMEM((n_half, 3, own, columns), wire),
            pltpu.VMEM((n_half - 1, 3, own, columns), wire),
            dma((n_atom,)),
            dma((n_atom,)),
            dma((n_atom - 1,)),
            dma((n_atom - 1,)),
            dma((n_half - 1,)),
            dma((n_half - 1,)),
        ],
        compiler_params=pltpu.CompilerParams(
            collective_id=0, has_side_effects=True, vmem_limit_bytes=60 * 2**20
        ),
        cost_estimate=pl.CostEstimate(
            flops=2 * 9 * rows * modes * columns,
            bytes_accessed=9 * rows * columns * 2,
            transcendentals=0,
        ),
        name="reduce",
    )(panel, images)
    return out.transpose(1, 0, 2)


def body(first_panel, second_panel, offsets, forces, displacements):
    groups = lax.axis_size("mode")
    rows_dev = first_panel.shape[0] // groups
    atoms_all = first_panel.shape[0] * lax.axis_size("atom")
    scale = 1.0 / (3.0 * atoms_all) ** 0.5
    padded = exchange_with_rims(second_panel.transpose(1, 0, 2))
    ordered, padded = lax.optimization_barrier((first_panel.transpose(1, 0, 2), padded))
    panel_rows = lax.all_to_all(ordered, "mode", split_axis=1, concat_axis=2, tiled=True)
    row_start = lax.axis_index("mode") * rows_dev
    shifts = lax.dynamic_slice_in_dim(offsets, row_start, rows_dev, 1)
    force_part = lax.dynamic_slice_in_dim(forces, row_start, rows_dev, 3)
    disp_part = lax.dynamic_slice_in_dim(displacements, row_start, rows_dev, 2)
    coef = merged_blocks(shifts, force_part, disp_part)
    images = make_images(padded, shifts, coef)
    return multiply_and_reduce(panel_rows, images, scale)


def solution(mesh):
    in_specs = (
        P("atom", None, "mode"),
        P("atom", None, "mode"),
        P(None, "atom"),
        P(None, None, None, "atom"),
        P(None, None, "atom"),
    )
    out_specs = P(("atom", "mode"), None, None)
    return jax.shard_map(body, mesh=mesh, in_specs=in_specs, out_specs=out_specs, check_vma=False)
```

```python
import functools

import jax
import jax.numpy as jnp
from jax import lax
from jax.experimental import pallas as pl
from jax.experimental.pallas import tpu as pltpu
from jax.sharding import PartitionSpec as P

RIM = 256
BLOCK = 128
CHUNK = 64
MESH = pl.DeviceIdType.MESH


def with_rims(block, width):
    axes = ("atom", "mode")
    count = lax.axis_size(axes)
    forward = [(i, (i + 1) % count) for i in range(count)]
    backward = [(target, source) for source, target in forward]
    low = lax.ppermute(block[:, block.shape[1] - width :], axes, forward)
    high = lax.ppermute(block[:, :width], axes, backward)
    return jnp.concatenate([low, block, high], axis=1)


def exchange_kernel(
    n_atom, groups, s_ref, out_ref, send, recv, rim_send, rim_recv, local
):
    me_atom = lax.axis_index("atom")
    me = lax.axis_index("mode")
    width = s_ref.shape[2]
    rows = s_ref.shape[1] // groups
    number = me_atom * groups + me
    count = n_atom * groups
    after = lax.rem(number + 1, count)
    before = lax.rem(number + count - 1, count)
    after = (after // groups, lax.rem(after, groups))
    before = (before // groups, lax.rem(before, groups))

    barrier = pltpu.get_barrier_semaphore()
    for s in range(1, groups):
        to = lax.rem(me + s, groups)
        pl.semaphore_signal(barrier, inc=1, device_id=(me_atom, to), device_id_type=MESH)
    pl.semaphore_signal(barrier, inc=1, device_id=after, device_id_type=MESH)
    pl.semaphore_signal(barrier, inc=1, device_id=before, device_id_type=MESH)
    pl.semaphore_wait(barrier, groups + 1)

    columns = pl.ds(pl.multiple_of(me * width, width), width)
    landing = out_ref.at[:, pl.ds(RIM, rows), columns]
    copies = []
    for s in range(1, groups):
        to = lax.rem(me + s, groups)
        copy = pltpu.make_async_remote_copy(
            src_ref=s_ref.at[:, pl.ds(pl.multiple_of(to * rows, rows), rows), :],
            dst_ref=landing,
            send_sem=send.at[s - 1],
            recv_sem=recv.at[s - 1],
            device_id=(me_atom, to),
            device_id_type=MESH,
        )
        copy.start()
        copies.append(copy)
    mine = pltpu.make_async_copy(
        s_ref.at[:, pl.ds(pl.multiple_of(me * rows, rows), rows), :], landing, local
    )
    mine.start()
    mine.wait()
    for copy in copies:
        copy.wait_recv()

    rims = []
    for at, (source, target, device) in enumerate(
        ((rows, 0, after), (RIM, RIM + rows, before))
    ):
        copy = pltpu.make_async_remote_copy(
            src_ref=out_ref.at[:, pl.ds(source, RIM), :],
            dst_ref=out_ref.at[:, pl.ds(target, RIM), :],
            send_sem=rim_send.at[at],
            recv_sem=rim_recv.at[at],
            device_id=device,
            device_id_type=MESH,
        )
        copy.start()
        rims.append(copy)
    for copy in rims:
        copy.wait_recv()
    for copy in copies + rims:
        copy.wait_send()


def exchange_with_rims(panel):
    n_atom, groups = lax.axis_size("atom"), lax.axis_size("mode")
    rows, width = panel.shape[1] // groups, panel.shape[2]
    if width % 128:
        whole = lax.all_to_all(panel, "mode", split_axis=1, concat_axis=2, tiled=True)
        return with_rims(whole, RIM)
    dma = pltpu.SemaphoreType.DMA
    return pl.pallas_call(
        functools.partial(exchange_kernel, n_atom, groups),
        out_shape=jax.ShapeDtypeStruct((3, rows + 2 * RIM, width * groups), panel.dtype),
        in_specs=[pl.BlockSpec(memory_space=pl.ANY)],
        out_specs=pl.BlockSpec(memory_space=pl.ANY),
        scratch_shapes=[dma((groups - 1,)), dma((groups - 1,)), dma((2,)), dma((2,)), dma],
        compiler_params=pltpu.CompilerParams(collective_id=1, has_side_effects=True),
        name="exchange",
    )(panel)


def merged_blocks(offsets, forces, displacements):
    slots, rows = offsets.shape
    blocks = displacements[:, :, None, None, :] * forces[:, None, :, :, :]
    blocks = blocks.astype(jnp.bfloat16).astype(jnp.float32).reshape(slots, 9, 3, rows)
    same = offsets[:, None, :] == offsets[None, :, :]
    merged = jnp.sum(
        jnp.where(same[:, :, None, None, :], blocks[None], 0.0), axis=1
    )
    return merged.transpose(1, 0, 2, 3).reshape(9, slots * 3, rows)


def panel_copies(groups, f_ref, panel_ref, send, recv, local):
    me_atom = lax.axis_index("atom")
    me = lax.axis_index("mode")
    width = f_ref.shape[2]
    rows = panel_ref.shape[1]
    landing = panel_ref.at[:, :, pl.ds(pl.multiple_of(me * width, width), width)]
    mine = pltpu.make_async_copy(
        f_ref.at[:, pl.ds(pl.multiple_of(me * rows, rows), rows), :], landing, local
    )
    copies = []
    for s in range(1, groups):
        to = lax.rem(me + s, groups)
        copies.append(
            pltpu.make_async_remote_copy(
                src_ref=f_ref.at[:, pl.ds(pl.multiple_of(to * rows, rows), rows), :],
                dst_ref=landing,
                send_sem=send.at[s - 1],
                recv_sem=recv.at[s - 1],
                device_id=(me_atom, to),
                device_id_type=MESH,
            )
        )
    return mine, copies


def image_panel_kernel(
    slots, groups, offs_ref, coef_ref, s_ref, f_ref, out_ref, panel_ref, w_ref, send, recv, local
):
    @pl.when(pl.program_id(0) == 0)
    def _():
        me_atom = lax.axis_index("atom")
        me = lax.axis_index("mode")
        barrier = pltpu.get_barrier_semaphore()
        for s in range(1, groups):
            to = lax.rem(me + s, groups)
            pl.semaphore_signal(barrier, inc=1, device_id=(me_atom, to), device_id_type=MESH)
        pl.semaphore_wait(barrier, groups - 1)
        mine, copies = panel_copies(groups, f_ref, panel_ref, send, recv, local)
        for copy in copies:
            copy.start()
        mine.start()

    image_kernel(slots, offs_ref, coef_ref, s_ref, out_ref, w_ref)

    @pl.when(pl.program_id(0) == pl.num_programs(0) - 1)
    def _():
        mine, copies = panel_copies(groups, f_ref, panel_ref, send, recv, local)
        mine.wait()
        for copy in copies:
            copy.wait()


def make_images_and_panel(padded, offs, coef, panel):
    slots, rows = offs.shape
    columns = padded.shape[2]
    window = BLOCK + 2 * RIM
    groups = lax.axis_size("mode")
    width = panel.shape[2]
    dma = pltpu.SemaphoreType.DMA
    return pl.pallas_call(
        functools.partial(image_panel_kernel, slots, groups),
        grid=(rows // BLOCK,),
        out_shape=(
            jax.ShapeDtypeStruct((9, rows, columns), jnp.bfloat16),
            jax.ShapeDtypeStruct((3, rows, groups * width), panel.dtype),
        ),
        in_specs=[
            pl.BlockSpec((slots, BLOCK), lambda i: (0, i)),
            pl.BlockSpec((9, slots * 3, BLOCK), lambda i: (0, 0, i)),
            pl.BlockSpec(memory_space=pltpu.VMEM),
            pl.BlockSpec(memory_space=pl.ANY),
        ],
        out_specs=(
            pl.BlockSpec((9, BLOCK, columns), lambda i: (0, i, 0)),
            pl.BlockSpec(memory_space=pl.ANY),
        ),
        scratch_shapes=[
            pltpu.VMEM((3, window, 9 * BLOCK), jnp.bfloat16),
            dma((groups - 1,)),
            dma((groups - 1,)),
            dma,
        ],
        compiler_params=pltpu.CompilerParams(
            collective_id=2, has_side_effects=True, vmem_limit_bytes=56 * 2**20
        ),
        name="images_panel",
    )(offs, coef, padded, panel)


def image_kernel(slots, offs_ref, coef_ref, s_ref, out_ref, w_ref):
    window = BLOCK + 2 * RIM
    start = pl.multiple_of(pl.program_id(0) * BLOCK, BLOCK)
    target = offs_ref[...] + lax.broadcasted_iota(jnp.int32, offs_ref.shape, 1) + RIM
    rows = lax.broadcasted_iota(jnp.int32, (CHUNK, BLOCK), 0)

    for qa in range(9):

        @pl.loop(0, window // CHUNK)
        def _(c):
            at = pl.multiple_of(c * CHUNK, CHUNK)
            here = rows + at
            acc = [jnp.zeros((CHUNK, BLOCK), jnp.float32) for _ in range(3)]
            for k in range(slots):
                hit = here == target[k : k + 1, :]
                for b in range(3):
                    row = coef_ref[qa, 3 * k + b : 3 * k + b + 1, :]
                    acc[b] = jnp.where(hit, row, acc[b])
            for b in range(3):
                w_ref[b, pl.ds(at, CHUNK), qa * BLOCK : (qa + 1) * BLOCK] = acc[b].astype(
                    jnp.bfloat16
                )

    columns = s_ref.shape[2]
    wide = 512

    @pl.loop(0, columns // wide)
    def _(c):
        at = pl.multiple_of(c * wide, wide)
        total = None
        for b in range(3):
            term = lax.dot_general(
                w_ref[b],
                s_ref[b, pl.ds(start, window), pl.ds(at, wide)],
                (((0,), (0,)), ((), ())),
                preferred_element_type=jnp.float32,
            )
            total = term if total is None else total + term
        out_ref[:, :, pl.ds(at, wide)] = total.astype(jnp.bfloat16).reshape(9, BLOCK, wide)


def make_images(padded, offs, coef):
    slots, rows = offs.shape
    columns = padded.shape[2]
    window = BLOCK + 2 * RIM
    return pl.pallas_call(
        functools.partial(image_kernel, slots),
        grid=(rows // BLOCK,),
        out_shape=jax.ShapeDtypeStruct((9, rows, columns), jnp.bfloat16),
        in_specs=[
            pl.BlockSpec((slots, BLOCK), lambda i: (0, i)),
            pl.BlockSpec((9, slots * 3, BLOCK), lambda i: (0, 0, i)),
            pl.BlockSpec(memory_space=pltpu.VMEM),
        ],
        out_specs=pl.BlockSpec((9, BLOCK, columns), lambda i: (0, i, 0)),
        scratch_shapes=[pltpu.VMEM((3, window, 9 * BLOCK), jnp.bfloat16)],
        compiler_params=pltpu.CompilerParams(vmem_limit_bytes=56 * 2**20),
        cost_estimate=pl.CostEstimate(
            flops=2 * 27 * rows * window * columns,
            bytes_accessed=9 * rows * columns * 2,
            transcendentals=0,
        ),
        name="images",
    )(offs, coef, padded)


def reduce_kernel(
    scale, n_atom, n_half, f_ref, img_ref, out_ref,
    part, core_in, atom_out, atom_in, z_out, z_in,
    core_send, core_recv, atom_send, atom_recv, z_send, z_recv,
):
    me_atom = lax.axis_index("atom")
    me_mode = lax.axis_index("mode")
    core = lax.rem(me_mode, 2)
    me_z = me_mode // 2
    other = me_z * 2 + 1 - core
    own = out_ref.shape[1]
    columns = img_ref.shape[3]
    chunk = n_half * 2 * own

    barrier = pltpu.get_barrier_semaphore()
    pl.semaphore_signal(barrier, inc=1, device_id=(me_atom, other), device_id_type=MESH)
    for s in range(1, n_atom):
        to = lax.rem(me_atom + s, n_atom)
        pl.semaphore_signal(barrier, inc=1, device_id=(to, me_mode), device_id_type=MESH)
    for s in range(1, n_half):
        to = lax.rem(me_z + s, n_half) * 2 + core
        pl.semaphore_signal(barrier, inc=1, device_id=(me_atom, to), device_id_type=MESH)
    pl.semaphore_wait(barrier, n_atom + n_half - 1)

    core_copies, atom_copies = [], []

    def multiply(s):
        a_to = lax.rem(me_atom + 1 + s, n_atom)

        @pl.loop(0, 3)
        def _(q):
            total = None
            for a in range(3):
                term = lax.dot_general(
                    f_ref[a, :, pl.ds(pl.multiple_of(a_to * chunk, chunk), chunk)],
                    img_ref[q, a],
                    (((0,), (0,)), ((), ())),
                    preferred_element_type=jnp.float32,
                )
                total = term if total is None else total + term
            total = (total * scale).astype(part.dtype)
            part[s, q] = total.reshape(n_half, 2, own, columns)

        copy = pltpu.make_async_remote_copy(
            src_ref=part.at[s, :, :, 1 - core],
            dst_ref=core_in.at[s],
            send_sem=core_send.at[s],
            recv_sem=core_recv.at[s],
            device_id=(me_atom, other),
            device_id_type=MESH,
        )
        copy.start()
        core_copies.append(copy)

    def combine(s):
        core_copies[s].wait_recv()

        @pl.loop(0, n_half)
        def _(h):
            for q in range(3):
                mine = part[s, q, h, core].astype(jnp.float32)
                atom_out[s, q, h] = (mine + core_in[s, q, h].astype(jnp.float32)).astype(
                    atom_out.dtype
                )

        if s < n_atom - 1:
            a_to = lax.rem(me_atom + 1 + s, n_atom)
            copy = pltpu.make_async_remote_copy(
                src_ref=atom_out.at[s],
                dst_ref=atom_in.at[s],
                send_sem=atom_send.at[s],
                recv_sem=atom_recv.at[s],
                device_id=(a_to, me_mode),
                device_id_type=MESH,
            )
            copy.start()
            atom_copies.append(copy)

    for s in range(n_atom):
        multiply(s)
        if s >= 1:
            combine(s - 1)
    combine(n_atom - 1)

    for copy in atom_copies:
        copy.wait_recv()
    z_copies = []
    for s in range(n_half):
        h = lax.rem(me_z + 1 + s, n_half)
        for q in range(3):
            total = atom_out[n_atom - 1, q, h].astype(jnp.float32)
            for t in range(n_atom - 1):
                total = total + atom_in[t, q, h].astype(jnp.float32)
            z_out[s, q] = total.astype(z_out.dtype)
        if s < n_half - 1:
            copy = pltpu.make_async_remote_copy(
                src_ref=z_out.at[s],
                dst_ref=z_in.at[s],
                send_sem=z_send.at[s],
                recv_sem=z_recv.at[s],
                device_id=(me_atom, h * 2 + core),
                device_id_type=MESH,
            )
            copy.start()
            z_copies.append(copy)
    for copy in z_copies:
        copy.wait_recv()
    for q in range(3):
        total = z_out[n_half - 1, q].astype(jnp.float32)
        for t in range(n_half - 1):
            total = total + z_in[t, q].astype(jnp.float32)
        out_ref[q] = total
    for copy in core_copies + atom_copies + z_copies:
        copy.wait_send()


def multiply_and_reduce(panel, images, scale):
    n_atom = lax.axis_size("atom")
    n_half = lax.axis_size("mode") // 2
    modes = panel.shape[2]
    columns = images.shape[2]
    rows = panel.shape[1]
    own = modes // (n_atom * n_half * 2)
    wire = jnp.bfloat16 if own % 16 == 0 else jnp.float32
    images = images.reshape(3, 3, rows, columns)
    vmem = pl.BlockSpec(memory_space=pltpu.VMEM)
    dma = pltpu.SemaphoreType.DMA
    out = pl.pallas_call(
        functools.partial(reduce_kernel, scale, n_atom, n_half),
        out_shape=jax.ShapeDtypeStruct((3, own, columns), jnp.float32),
        in_specs=[vmem, vmem],
        out_specs=vmem,
        scratch_shapes=[
            pltpu.VMEM((n_atom, 3, n_half, 2, own, columns), wire),
            pltpu.VMEM((n_atom, 3, n_half, own, columns), wire),
            pltpu.VMEM((n_atom, 3, n_half, own, columns), wire),
            pltpu.VMEM((n_atom - 1, 3, n_half, own, columns), wire),
            pltpu.VMEM((n_half, 3, own, columns), wire),
            pltpu.VMEM((n_half - 1, 3, own, columns), wire),
            dma((n_atom,)),
            dma((n_atom,)),
            dma((n_atom - 1,)),
            dma((n_atom - 1,)),
            dma((n_half - 1,)),
            dma((n_half - 1,)),
        ],
        compiler_params=pltpu.CompilerParams(
            collective_id=0, has_side_effects=True, vmem_limit_bytes=60 * 2**20
        ),
        cost_estimate=pl.CostEstimate(
            flops=2 * 9 * rows * modes * columns,
            bytes_accessed=9 * rows * columns * 2,
            transcendentals=0,
        ),
        name="reduce",
    )(panel, images)
    return out.transpose(1, 0, 2)


def body(first_panel, second_panel, offsets, forces, displacements):
    groups = lax.axis_size("mode")
    rows_dev = first_panel.shape[0] // groups
    atoms_all = first_panel.shape[0] * lax.axis_size("atom")
    scale = 1.0 / (3.0 * atoms_all) ** 0.5
    padded = exchange_with_rims(second_panel.transpose(1, 0, 2))
    row_start = lax.axis_index("mode") * rows_dev
    shifts = lax.dynamic_slice_in_dim(offsets, row_start, rows_dev, 1)
    force_part = lax.dynamic_slice_in_dim(forces, row_start, rows_dev, 3)
    disp_part = lax.dynamic_slice_in_dim(displacements, row_start, rows_dev, 2)
    coef = merged_blocks(shifts, force_part, disp_part)
    ordered = first_panel.transpose(1, 0, 2)
    if ordered.shape[2] % 128:
        ordered, padded = lax.optimization_barrier((ordered, padded))
        panel_rows = lax.all_to_all(ordered, "mode", split_axis=1, concat_axis=2, tiled=True)
        images = make_images(padded, shifts, coef)
    else:
        images, panel_rows = make_images_and_panel(padded, shifts, coef, ordered)
    return multiply_and_reduce(panel_rows, images, scale)


def solution(mesh):
    in_specs = (
        P("atom", None, "mode"),
        P("atom", None, "mode"),
        P(None, "atom"),
        P(None, None, None, "atom"),
        P(None, None, "atom"),
    )
    out_specs = P(("atom", "mode"), None, None)
    return jax.shard_map(body, mesh=mesh, in_specs=in_specs, out_specs=out_specs, check_vma=False)
```

```python
import functools

import jax
import jax.numpy as jnp
from jax import lax
from jax.experimental import pallas as pl
from jax.experimental.pallas import tpu as pltpu
from jax.sharding import PartitionSpec as P

RIM = 256
BLOCK = 128
CHUNK = 64
MESH = pl.DeviceIdType.MESH


def with_rims(block, width):
    axes = ("atom", "mode")
    count = lax.axis_size(axes)
    forward = [(i, (i + 1) % count) for i in range(count)]
    backward = [(target, source) for source, target in forward]
    low = lax.ppermute(block[:, block.shape[1] - width :], axes, forward)
    high = lax.ppermute(block[:, :width], axes, backward)
    return jnp.concatenate([low, block, high], axis=1)


def exchange_kernel(
    n_atom, groups, s_ref, offs_ref, block_ref, out_ref, coef_ref,
    send, recv, rim_send, rim_recv, local,
):
    me_atom = lax.axis_index("atom")
    me = lax.axis_index("mode")
    width = s_ref.shape[2]
    rows = s_ref.shape[1] // groups
    number = me_atom * groups + me
    count = n_atom * groups
    after = lax.rem(number + 1, count)
    before = lax.rem(number + count - 1, count)
    after = (after // groups, lax.rem(after, groups))
    before = (before // groups, lax.rem(before, groups))

    barrier = pltpu.get_barrier_semaphore()
    for s in range(1, groups):
        to = lax.rem(me + s, groups)
        pl.semaphore_signal(barrier, inc=1, device_id=(me_atom, to), device_id_type=MESH)
    pl.semaphore_signal(barrier, inc=1, device_id=after, device_id_type=MESH)
    pl.semaphore_signal(barrier, inc=1, device_id=before, device_id_type=MESH)
    pl.semaphore_wait(barrier, groups + 1)

    columns = pl.ds(pl.multiple_of(me * width, width), width)
    landing = out_ref.at[:, pl.ds(RIM, rows), columns]
    copies = []
    for s in range(1, groups):
        to = lax.rem(me + s, groups)
        copy = pltpu.make_async_remote_copy(
            src_ref=s_ref.at[:, pl.ds(pl.multiple_of(to * rows, rows), rows), :],
            dst_ref=landing,
            send_sem=send.at[s - 1],
            recv_sem=recv.at[s - 1],
            device_id=(me_atom, to),
            device_id_type=MESH,
        )
        copy.start()
        copies.append(copy)
    mine = pltpu.make_async_copy(
        s_ref.at[:, pl.ds(pl.multiple_of(me * rows, rows), rows), :], landing, local
    )
    mine.start()

    slots = offs_ref.shape[0]

    @pl.loop(0, slots)
    def _(k):
        here = offs_ref[pl.ds(k, 1), :]

        def add(j, total):
            same = offs_ref[pl.ds(j, 1), :] == here
            return total + jnp.where(same, block_ref[j], 0.0)

        coef_ref[k] = lax.fori_loop(0, slots, add, jnp.zeros(coef_ref.shape[1:], jnp.float32))

    mine.wait()
    for copy in copies:
        copy.wait_recv()

    rims = []
    for at, (source, target, device) in enumerate(
        ((rows, 0, after), (RIM, RIM + rows, before))
    ):
        copy = pltpu.make_async_remote_copy(
            src_ref=out_ref.at[:, pl.ds(source, RIM), :],
            dst_ref=out_ref.at[:, pl.ds(target, RIM), :],
            send_sem=rim_send.at[at],
            recv_sem=rim_recv.at[at],
            device_id=device,
            device_id_type=MESH,
        )
        copy.start()
        rims.append(copy)
    for copy in rims:
        copy.wait_recv()
    for copy in copies + rims:
        copy.wait_send()


def exchange_with_rims(panel, offs, blocks):
    n_atom, groups = lax.axis_size("atom"), lax.axis_size("mode")
    rows, width = panel.shape[1] // groups, panel.shape[2]
    if width % 128:
        whole = lax.all_to_all(panel, "mode", split_axis=1, concat_axis=2, tiled=True)
        return with_rims(whole, RIM), merged_blocks(offs, blocks)
    vmem = pl.BlockSpec(memory_space=pltpu.VMEM)
    dma = pltpu.SemaphoreType.DMA
    return pl.pallas_call(
        functools.partial(exchange_kernel, n_atom, groups),
        out_shape=(
            jax.ShapeDtypeStruct((3, rows + 2 * RIM, width * groups), panel.dtype),
            jax.ShapeDtypeStruct(blocks.shape, jnp.float32),
        ),
        in_specs=[pl.BlockSpec(memory_space=pl.ANY), vmem, vmem],
        out_specs=(pl.BlockSpec(memory_space=pl.ANY), vmem),
        scratch_shapes=[dma((groups - 1,)), dma((groups - 1,)), dma((2,)), dma((2,)), dma],
        compiler_params=pltpu.CompilerParams(collective_id=1, has_side_effects=True),
        name="exchange",
    )(panel, offs, blocks)


def rounded_blocks(forces, displacements):
    blocks = displacements[:, :, None, None, :] * forces[:, None, :, :, :]
    slots, rows = blocks.shape[0], blocks.shape[4]
    return blocks.astype(jnp.bfloat16).astype(jnp.float32).reshape(slots, 27, rows)


def merged_blocks(offsets, blocks):
    same = offsets[:, None, :] == offsets[None, :, :]
    return jnp.sum(jnp.where(same[:, :, None, :], blocks[None], 0.0), axis=1)


def panel_copies(groups, f_ref, panel_ref, send, recv, local):
    me_atom = lax.axis_index("atom")
    me = lax.axis_index("mode")
    width = f_ref.shape[2]
    rows = panel_ref.shape[1]
    landing = panel_ref.at[:, :, pl.ds(pl.multiple_of(me * width, width), width)]
    mine = pltpu.make_async_copy(
        f_ref.at[:, pl.ds(pl.multiple_of(me * rows, rows), rows), :], landing, local
    )
    copies = []
    for s in range(1, groups):
        to = lax.rem(me + s, groups)
        copies.append(
            pltpu.make_async_remote_copy(
                src_ref=f_ref.at[:, pl.ds(pl.multiple_of(to * rows, rows), rows), :],
                dst_ref=landing,
                send_sem=send.at[s - 1],
                recv_sem=recv.at[s - 1],
                device_id=(me_atom, to),
                device_id_type=MESH,
            )
        )
    return mine, copies


def image_panel_kernel(
    slots, groups, offs_ref, coef_ref, s_ref, f_ref, out_ref, panel_ref, w_ref, send, recv, local
):
    @pl.when(pl.program_id(0) == 0)
    def _():
        me_atom = lax.axis_index("atom")
        me = lax.axis_index("mode")
        barrier = pltpu.get_barrier_semaphore()
        for s in range(1, groups):
            to = lax.rem(me + s, groups)
            pl.semaphore_signal(barrier, inc=1, device_id=(me_atom, to), device_id_type=MESH)
        pl.semaphore_wait(barrier, groups - 1)
        mine, copies = panel_copies(groups, f_ref, panel_ref, send, recv, local)
        for copy in copies:
            copy.start()
        mine.start()

    image_kernel(slots, offs_ref, coef_ref, s_ref, out_ref, w_ref)

    @pl.when(pl.program_id(0) == pl.num_programs(0) - 1)
    def _():
        mine, copies = panel_copies(groups, f_ref, panel_ref, send, recv, local)
        mine.wait()
        for copy in copies:
            copy.wait()


def make_images_and_panel(padded, offs, coef, panel):
    slots, rows = offs.shape
    columns = padded.shape[2]
    window = BLOCK + 2 * RIM
    groups = lax.axis_size("mode")
    width = panel.shape[2]
    dma = pltpu.SemaphoreType.DMA
    return pl.pallas_call(
        functools.partial(image_panel_kernel, slots, groups),
        grid=(rows // BLOCK,),
        out_shape=(
            jax.ShapeDtypeStruct((9, rows, columns), jnp.bfloat16),
            jax.ShapeDtypeStruct((3, rows, groups * width), panel.dtype),
        ),
        in_specs=[
            pl.BlockSpec((slots, BLOCK), lambda i: (0, i)),
            pl.BlockSpec((slots, 27, BLOCK), lambda i: (0, 0, i)),
            pl.BlockSpec(memory_space=pltpu.VMEM),
            pl.BlockSpec(memory_space=pl.ANY),
        ],
        out_specs=(
            pl.BlockSpec((9, BLOCK, columns), lambda i: (0, i, 0)),
            pl.BlockSpec(memory_space=pl.ANY),
        ),
        scratch_shapes=[
            pltpu.VMEM((3, window, 9 * BLOCK), jnp.bfloat16),
            dma((groups - 1,)),
            dma((groups - 1,)),
            dma,
        ],
        compiler_params=pltpu.CompilerParams(
            collective_id=2, has_side_effects=True, vmem_limit_bytes=56 * 2**20
        ),
        name="images_panel",
    )(offs, coef, padded, panel)


def image_kernel(slots, offs_ref, coef_ref, s_ref, out_ref, w_ref):
    window = BLOCK + 2 * RIM
    start = pl.multiple_of(pl.program_id(0) * BLOCK, BLOCK)
    target = offs_ref[...] + lax.broadcasted_iota(jnp.int32, offs_ref.shape, 1) + RIM
    rows = lax.broadcasted_iota(jnp.int32, (CHUNK, BLOCK), 0)

    for qa in range(9):

        @pl.loop(0, window // CHUNK)
        def _(c):
            at = pl.multiple_of(c * CHUNK, CHUNK)
            here = rows + at
            acc = [jnp.zeros((CHUNK, BLOCK), jnp.float32) for _ in range(3)]
            for k in range(slots):
                hit = here == target[k : k + 1, :]
                for b in range(3):
                    row = coef_ref[k, 3 * qa + b : 3 * qa + b + 1, :]
                    acc[b] = jnp.where(hit, row, acc[b])
            for b in range(3):
                w_ref[b, pl.ds(at, CHUNK), qa * BLOCK : (qa + 1) * BLOCK] = acc[b].astype(
                    jnp.bfloat16
                )

    columns = s_ref.shape[2]
    wide = 512

    @pl.loop(0, columns // wide)
    def _(c):
        at = pl.multiple_of(c * wide, wide)
        total = None
        for b in range(3):
            term = lax.dot_general(
                w_ref[b],
                s_ref[b, pl.ds(start, window), pl.ds(at, wide)],
                (((0,), (0,)), ((), ())),
                preferred_element_type=jnp.float32,
            )
            total = term if total is None else total + term
        out_ref[:, :, pl.ds(at, wide)] = total.astype(jnp.bfloat16).reshape(9, BLOCK, wide)


def make_images(padded, offs, coef):
    slots, rows = offs.shape
    columns = padded.shape[2]
    window = BLOCK + 2 * RIM
    return pl.pallas_call(
        functools.partial(image_kernel, slots),
        grid=(rows // BLOCK,),
        out_shape=jax.ShapeDtypeStruct((9, rows, columns), jnp.bfloat16),
        in_specs=[
            pl.BlockSpec((slots, BLOCK), lambda i: (0, i)),
            pl.BlockSpec((slots, 27, BLOCK), lambda i: (0, 0, i)),
            pl.BlockSpec(memory_space=pltpu.VMEM),
        ],
        out_specs=pl.BlockSpec((9, BLOCK, columns), lambda i: (0, i, 0)),
        scratch_shapes=[pltpu.VMEM((3, window, 9 * BLOCK), jnp.bfloat16)],
        compiler_params=pltpu.CompilerParams(vmem_limit_bytes=56 * 2**20),
        cost_estimate=pl.CostEstimate(
            flops=2 * 27 * rows * window * columns,
            bytes_accessed=9 * rows * columns * 2,
            transcendentals=0,
        ),
        name="images",
    )(offs, coef, padded)


def reduce_kernel(
    scale, n_atom, n_half, f_ref, img_ref, out_ref,
    part, core_in, atom_out, atom_in, z_out, z_in,
    core_send, core_recv, atom_send, atom_recv, z_send, z_recv,
):
    me_atom = lax.axis_index("atom")
    me_mode = lax.axis_index("mode")
    core = lax.rem(me_mode, 2)
    me_z = me_mode // 2
    other = me_z * 2 + 1 - core
    own = out_ref.shape[1]
    columns = img_ref.shape[3]
    chunk = n_half * 2 * own

    barrier = pltpu.get_barrier_semaphore()
    pl.semaphore_signal(barrier, inc=1, device_id=(me_atom, other), device_id_type=MESH)
    for s in range(1, n_atom):
        to = lax.rem(me_atom + s, n_atom)
        pl.semaphore_signal(barrier, inc=1, device_id=(to, me_mode), device_id_type=MESH)
    for s in range(1, n_half):
        to = lax.rem(me_z + s, n_half) * 2 + core
        pl.semaphore_signal(barrier, inc=1, device_id=(me_atom, to), device_id_type=MESH)
    pl.semaphore_wait(barrier, n_atom + n_half - 1)

    core_copies, atom_copies = [], []

    def multiply(s):
        a_to = lax.rem(me_atom + 1 + s, n_atom)

        @pl.loop(0, 3)
        def _(q):
            total = None
            for a in range(3):
                term = lax.dot_general(
                    f_ref[a, :, pl.ds(pl.multiple_of(a_to * chunk, chunk), chunk)],
                    img_ref[q, a],
                    (((0,), (0,)), ((), ())),
                    preferred_element_type=jnp.float32,
                )
                total = term if total is None else total + term
            total = (total * scale).astype(part.dtype)
            part[s, q] = total.reshape(n_half, 2, own, columns)

        copy = pltpu.make_async_remote_copy(
            src_ref=part.at[s, :, :, 1 - core],
            dst_ref=core_in.at[s],
            send_sem=core_send.at[s],
            recv_sem=core_recv.at[s],
            device_id=(me_atom, other),
            device_id_type=MESH,
        )
        copy.start()
        core_copies.append(copy)

    def combine(s):
        core_copies[s].wait_recv()

        @pl.loop(0, n_half)
        def _(h):
            for q in range(3):
                mine = part[s, q, h, core].astype(jnp.float32)
                atom_out[s, q, h] = (mine + core_in[s, q, h].astype(jnp.float32)).astype(
                    atom_out.dtype
                )

        if s < n_atom - 1:
            a_to = lax.rem(me_atom + 1 + s, n_atom)
            copy = pltpu.make_async_remote_copy(
                src_ref=atom_out.at[s],
                dst_ref=atom_in.at[s],
                send_sem=atom_send.at[s],
                recv_sem=atom_recv.at[s],
                device_id=(a_to, me_mode),
                device_id_type=MESH,
            )
            copy.start()
            atom_copies.append(copy)

    for s in range(n_atom):
        multiply(s)
        if s >= 1:
            combine(s - 1)
    combine(n_atom - 1)

    for copy in atom_copies:
        copy.wait_recv()
    z_copies = []
    for s in range(n_half):
        h = lax.rem(me_z + 1 + s, n_half)
        for q in range(3):
            total = atom_out[n_atom - 1, q, h].astype(jnp.float32)
            for t in range(n_atom - 1):
                total = total + atom_in[t, q, h].astype(jnp.float32)
            z_out[s, q] = total.astype(z_out.dtype)
        if s < n_half - 1:
            copy = pltpu.make_async_remote_copy(
                src_ref=z_out.at[s],
                dst_ref=z_in.at[s],
                send_sem=z_send.at[s],
                recv_sem=z_recv.at[s],
                device_id=(me_atom, h * 2 + core),
                device_id_type=MESH,
            )
            copy.start()
            z_copies.append(copy)
    for copy in z_copies:
        copy.wait_recv()
    for q in range(3):
        total = z_out[n_half - 1, q].astype(jnp.float32)
        for t in range(n_half - 1):
            total = total + z_in[t, q].astype(jnp.float32)
        out_ref[q] = total
    for copy in core_copies + atom_copies + z_copies:
        copy.wait_send()


def multiply_and_reduce(panel, images, scale):
    n_atom = lax.axis_size("atom")
    n_half = lax.axis_size("mode") // 2
    modes = panel.shape[2]
    columns = images.shape[2]
    rows = panel.shape[1]
    own = modes // (n_atom * n_half * 2)
    wire = jnp.bfloat16 if own % 16 == 0 else jnp.float32
    images = images.reshape(3, 3, rows, columns)
    vmem = pl.BlockSpec(memory_space=pltpu.VMEM)
    dma = pltpu.SemaphoreType.DMA
    out = pl.pallas_call(
        functools.partial(reduce_kernel, scale, n_atom, n_half),
        out_shape=jax.ShapeDtypeStruct((3, own, columns), jnp.float32),
        in_specs=[vmem, vmem],
        out_specs=vmem,
        scratch_shapes=[
            pltpu.VMEM((n_atom, 3, n_half, 2, own, columns), wire),
            pltpu.VMEM((n_atom, 3, n_half, own, columns), wire),
            pltpu.VMEM((n_atom, 3, n_half, own, columns), wire),
            pltpu.VMEM((n_atom - 1, 3, n_half, own, columns), wire),
            pltpu.VMEM((n_half, 3, own, columns), wire),
            pltpu.VMEM((n_half - 1, 3, own, columns), wire),
            dma((n_atom,)),
            dma((n_atom,)),
            dma((n_atom - 1,)),
            dma((n_atom - 1,)),
            dma((n_half - 1,)),
            dma((n_half - 1,)),
        ],
        compiler_params=pltpu.CompilerParams(
            collective_id=0, has_side_effects=True, vmem_limit_bytes=60 * 2**20
        ),
        cost_estimate=pl.CostEstimate(
            flops=2 * 9 * rows * modes * columns,
            bytes_accessed=9 * rows * columns * 2,
            transcendentals=0,
        ),
        name="reduce",
    )(panel, images)
    return out.transpose(1, 0, 2)


def body(first_panel, second_panel, offsets, forces, displacements):
    groups = lax.axis_size("mode")
    rows_dev = first_panel.shape[0] // groups
    atoms_all = first_panel.shape[0] * lax.axis_size("atom")
    scale = 1.0 / (3.0 * atoms_all) ** 0.5
    row_start = lax.axis_index("mode") * rows_dev
    shifts = lax.dynamic_slice_in_dim(offsets, row_start, rows_dev, 1)
    force_part = lax.dynamic_slice_in_dim(forces, row_start, rows_dev, 3)
    disp_part = lax.dynamic_slice_in_dim(displacements, row_start, rows_dev, 2)
    blocks = rounded_blocks(force_part, disp_part)
    padded, coef = exchange_with_rims(second_panel.transpose(1, 0, 2), shifts, blocks)
    ordered = first_panel.transpose(1, 0, 2)
    if ordered.shape[2] % 128:
        ordered, padded = lax.optimization_barrier((ordered, padded))
        panel_rows = lax.all_to_all(ordered, "mode", split_axis=1, concat_axis=2, tiled=True)
        images = make_images(padded, shifts, coef)
    else:
        images, panel_rows = make_images_and_panel(padded, shifts, coef, ordered)
    return multiply_and_reduce(panel_rows, images, scale)


def solution(mesh):
    in_specs = (
        P("atom", None, "mode"),
        P("atom", None, "mode"),
        P(None, "atom"),
        P(None, None, None, "atom"),
        P(None, None, "atom"),
    )
    out_specs = P(("atom", "mode"), None, None)
    return jax.shard_map(body, mesh=mesh, in_specs=in_specs, out_specs=out_specs, check_vma=False)
```
